32 devices in a mesh: seq: 8 (over z, x), grp: 4 (over y, core).
Axes of the slice: x: 2, y: 2, z: 4, core: 2. Of those that a mesh axis runs over, the one named last changes fastest.
Arguments:
- in_gate: bfloat16 [8192, 512], P(('grp', 'seq')), parts along dimension 0, may hold values from -6 to 6
- values: bfloat16 [8192, 512], P(('grp', 'seq')), parts along dimension 0, may hold values from -6 to 6
- out_gate: bfloat16 [8192, 512], P(('grp', 'seq')), parts along dimension 0, may hold values from -6 to 6
- filter_taps: bfloat16 [2048, 512], P('seq'), may hold values from -0.125 to 0.125
- skip_gain: float32 [512], replicated, may hold values from -4 to 4
Outputs:
- mixed: bfloat16 [8192, 512], P(('grp', 'seq')), parts along dimension 0
The draws below stay inside these ranges and needn't reach their ends.
There are 4 independent parts, one for each index of `grp`. The reference program is written for one: setup_inputs(seed, part) draws one part's arguments, and reference() takes and returns one part's arrays. A program takes and returns all parts, laid end to end along the dimension named above; an argument that names none is the same for every part. Nothing has to cross between parts.
All inputs are finite; a program needn't handle non-finite values.
Results may differ from the reference program's by a relative error of at most 0.001.
Values sent between devices are 32-bit elements; how exact they have to be, the bound alone decides.
A program may use at most 64 MiB of HBM per device.

```python
import jax
import jax.numpy as jnp

CH = 512
SEQ_LEN = 2048


def level_of(rng, extent, shards, smallest, largest):
    def one(axis_at, blocks):
        steps = jax.random.uniform(jax.random.fold_in(jax.random.fold_in(rng, 6), axis_at), (blocks,), jnp.float32, smallest / len(shards), largest / len(shards))
        return jnp.repeat(jnp.exp(steps), extent[axis_at] // blocks).reshape((-1,) + (1,) * (len(extent) - axis_at - 1))

    factor_of = one(*shards[0])
    for cut in shards[1:]:
        factor_of = factor_of * one(*cut)
    return factor_of


def noise(key, extent, deviation, reach, pieces=(), dtype=jnp.bfloat16):
    result = deviation * jax.random.normal(key, extent, jnp.float32)
    if pieces:
        result = result * level_of(key, extent, pieces, -0.22, 0.18)
    return jnp.clip(result, -reach, reach).astype(dtype)


def setup_inputs(seed: int = 0, part: int = 0) -> dict:
    streams_of = jax.random.split(jax.random.key(seed), 6)
    own_keys = jax.random.split(jax.random.fold_in(streams_of[5], part), 6)
    return {
        "in_gate": noise(own_keys[0], (SEQ_LEN, CH), 1.0, 6.0, ((0, 8),)),
        "values": noise(own_keys[1], (SEQ_LEN, CH), 1.0, 6.0, ((0, 8),)),
        "out_gate": noise(own_keys[2], (SEQ_LEN, CH), 1.0, 6.0, ((0, 8),)),
        "filter_taps": noise(streams_of[3], (SEQ_LEN, CH), SEQ_LEN ** -0.5, 0.125, ((0, 8),)),
        "skip_gain": noise(streams_of[4], (CH,), 1.0, 4.0, (), jnp.float32),
    }


def reference(in_gate, values, out_gate, filter_taps, skip_gain):
    gated = in_gate.astype(jnp.float32) * values.astype(jnp.float32)
    taps_real = filter_taps.astype(jnp.float32)
    padded = 2 * SEQ_LEN
    spectrum = jnp.fft.rfft(gated, n=padded, axis=0) * jnp.fft.rfft(taps_real, n=padded, axis=0)
    conv = jnp.fft.irfft(spectrum, n=padded, axis=0)[:SEQ_LEN]
    total = conv + skip_gain[None, :] * gated
    return (out_gate.astype(jnp.float32) * total).astype(jnp.bfloat16)
```

```python
import functools

import jax
import jax.numpy as jnp
from jax import lax
from jax.experimental import pallas as pl
from jax.experimental.pallas import tpu as pltpu
from jax.sharding import PartitionSpec as P

LANES = 128
COARSE = 16
FINE = 8
CHUNK = 16


def kernel(
    devices,
    in_gate,
    values,
    out_gate,
    taps,
    skip_gain,
    mixed,
    sent,
    held,
    block,
    turned,
    back,
    conv,
    send_sem,
    recv_sem,
    back_send_sem,
    back_recv_sem,
):
    own, channels = in_gate.shape
    share = channels // devices
    chunks = share // CHUNK
    per_owner = own // LANES
    count = per_owner * devices
    width = FINE * count
    me = lax.axis_index("seq")

    barrier = pltpu.get_barrier_semaphore()
    for step in range(1, devices):
        peer = lax.rem(me + step, devices)
        pl.semaphore_signal(
            barrier, inc=1, device_id={"seq": peer}, device_id_type=pl.DeviceIdType.MESH
        )

    flip = (
        lax.broadcasted_iota(jnp.int32, (own, own), 0)
        + lax.broadcasted_iota(jnp.int32, (own, own), 1)
        == own - 1
    )
    flip = flip.astype(jnp.float32).astype(jnp.bfloat16)
    taps_turned = taps[...].astype(jnp.float32).T.astype(jnp.bfloat16)
    taps_turned = jnp.dot(taps_turned, flip, preferred_element_type=jnp.float32)
    gated = in_gate[...].astype(jnp.float32) * values[...].astype(jnp.float32)
    gated = gated.T
    for u in range(per_owner):
        sent[0, u] = gated[:, u * LANES : (u + 1) * LANES]
        sent[1, u] = taps_turned[:, u * LANES : (u + 1) * LANES]

    pl.semaphore_wait(barrier, devices - 1)

    def rows_of(device, chunk):
        return pl.ds(pl.multiple_of(device * share + chunk * CHUNK, CHUNK), CHUNK)

    def forward(step, chunk):
        peer = lax.rem(me + step, devices)
        return pltpu.make_async_remote_copy(
            src_ref=sent.at[:, :, rows_of(peer, chunk), :],
            dst_ref=held.at[me, :, :, pl.ds(chunk * CHUNK, CHUNK), :],
            send_sem=send_sem.at[step, chunk],
            recv_sem=recv_sem.at[step, chunk],
            device_id={"seq": peer},
            device_id_type=pl.DeviceIdType.MESH,
        )

    def backward(step, chunk):
        peer = lax.rem(me + step, devices)
        return pltpu.make_async_remote_copy(
            src_ref=turned.at[chunk, owner_rows(peer), :],
            dst_ref=back.at[me * chunks + chunk],
            send_sem=back_send_sem.at[step, chunk],
            recv_sem=back_recv_sem.at[step, chunk],
            device_id={"seq": peer},
            device_id_type=pl.DeviceIdType.MESH,
        )

    def owner_rows(device):
        start = FINE * per_owner * (devices - 1 - device)
        return pl.ds(pl.multiple_of(start, FINE * per_owner), FINE * per_owner)

    for chunk in range(chunks):
        for step in range(1, devices):
            forward(step, chunk).start()
    for chunk in range(chunks):
        rows = slice(chunk * CHUNK, (chunk + 1) * CHUNK)
        held[me, :, :, rows, :] = sent[:, :, rows_of(me, chunk), :]

    coarse_row = lax.broadcasted_iota(jnp.int32, (COARSE, LANES), 0)
    coarse_lane = lax.broadcasted_iota(jnp.int32, (COARSE, LANES), 1)
    coarse_mask = coarse_lane >= FINE * coarse_row
    fine_row = lax.broadcasted_iota(jnp.int32, (FINE, LANES), 0)
    fine_lane = lax.broadcasted_iota(jnp.int32, (FINE, LANES), 1)
    fine_mask = fine_lane + (FINE - 1) - fine_row < LANES
    wide_lane = lax.broadcasted_iota(jnp.int32, (COARSE, width), 1)

    def convolve(chunk, at, carry):
        row = pl.ds(chunk * CHUNK + at, 1)
        pieces = []
        before = jnp.zeros((COARSE, LANES), jnp.float32)
        for m in range(count):
            line = held[m // per_owner, 0, m % per_owner, row, :]
            rolled = pltpu.roll(
                jnp.broadcast_to(line, (COARSE, LANES)), 0, 1, stride=FINE, stride_axis=0
            )
            shifted = jnp.where(coarse_mask, rolled, before)
            before = rolled
            high = shifted.astype(jnp.bfloat16)
            low = (shifted - high.astype(jnp.float32)).astype(jnp.bfloat16)
            pieces.append(jnp.concatenate([high, low], axis=1))
        signal = jnp.concatenate(pieces, axis=0)
        pieces = []
        after = jnp.zeros((FINE, LANES), jnp.float32)
        for b in range(count - 1, -1, -1):
            line = held[devices - 1 - b // per_owner, 1, b % per_owner, row, :]
            rolled = pltpu.roll(
                jnp.broadcast_to(line, (FINE, LANES)),
                LANES - FINE + 1,
                1,
                stride=1,
                stride_axis=0,
            )
            pieces.append(jnp.where(fine_mask, rolled, after))
            after = rolled
        filters = jnp.concatenate(pieces[::-1], axis=0).astype(jnp.bfloat16)
        filters = jnp.concatenate([filters, filters], axis=1)
        product = lax.dot_general(
            signal, filters, (((1,), (1,)), ((), ())), preferred_element_type=jnp.float32
        )
        total = product[0:COARSE]
        for m in range(1, count):
            part = product[m * COARSE : (m + 1) * COARSE]
            part = jnp.where(wide_lane >= FINE * m, part, 0.0)
            total = total + pltpu.roll(part, width - FINE * m, 1)
        for group in range(width // LANES):
            block[group, pl.ds(at, COARSE, stride=CHUNK), :] = total[
                :, group * LANES : (group + 1) * LANES
            ]
        return carry

    for chunk in range(chunks):
        for step in range(1, devices):
            forward(step, chunk).wait_recv()
        lax.fori_loop(0, CHUNK, functools.partial(convolve, chunk), 0)
        for group in range(width // LANES):
            turned[chunk, group * LANES : (group + 1) * LANES, :] = block[group].T
        for step in range(1, devices):
            backward(step, chunk).start()
        back[me * chunks + chunk] = turned[chunk, owner_rows(me), :]

    for chunk in range(chunks):
        for step in range(1, devices):
            forward(step, chunk).wait_send()
            backward(step, chunk).wait_send()
            backward(step, chunk).wait_recv()

    parts = LANES // CHUNK

    def place(group, carry):
        for a in range(COARSE):
            lanes = pl.ds(a * CHUNK, CHUNK)
            merged = jnp.concatenate(
                [back[group * parts + part, :, lanes] for part in range(parts)], axis=1
            )
            for u in range(per_owner):
                start = LANES * (per_owner - 1 - u) + FINE * (COARSE - 1 - a)
                conv[group, start : start + FINE, :] = merged[u * FINE : (u + 1) * FINE]
        return carry

    lax.fori_loop(0, channels // LANES, place, 0)
    for group in range(channels // LANES):
        lanes = slice(group * LANES, (group + 1) * LANES)
        gated = in_gate[:, lanes].astype(jnp.float32) * values[:, lanes].astype(jnp.float32)
        total = conv[group] + skip_gain[:, lanes] * gated
        mixed[:, lanes] = (out_gate[:, lanes].astype(jnp.float32) * total).astype(jnp.bfloat16)


def local(in_gate, values, out_gate, filter_taps, skip_gain):
    own, channels = in_gate.shape
    devices = lax.axis_size("seq")
    share = channels // devices
    chunks = share // CHUNK
    width = FINE * (own // LANES) * devices
    owned = FINE * (own // LANES)
    vmem = pl.BlockSpec(memory_space=pltpu.VMEM)
    return pl.pallas_call(
        functools.partial(kernel, devices),
        out_shape=jax.ShapeDtypeStruct((own, channels), jnp.bfloat16),
        in_specs=[vmem] * 5,
        out_specs=vmem,
        scratch_shapes=[
            pltpu.VMEM((2, own // LANES, channels, LANES), jnp.float32),
            pltpu.VMEM((devices, 2, own // LANES, share, LANES), jnp.float32),
            pltpu.VMEM((width // LANES, COARSE * CHUNK, LANES), jnp.float32),
            pltpu.VMEM((chunks, width, COARSE * CHUNK), jnp.float32),
            pltpu.VMEM((devices * chunks, owned, COARSE * CHUNK), jnp.float32),
            pltpu.VMEM((channels // LANES, own, LANES), jnp.float32),
            pltpu.SemaphoreType.DMA((devices, chunks)),
            pltpu.SemaphoreType.DMA((devices, chunks)),
            pltpu.SemaphoreType.DMA((devices, chunks)),
            pltpu.SemaphoreType.DMA((devices, chunks)),
        ],
        compiler_params=pltpu.CompilerParams(
            collective_id=0, has_side_effects=True, vmem_limit_bytes=40 * 1024 * 1024
        ),
    )(in_gate, values, out_gate, filter_taps, skip_gain.reshape(1, channels))


def solution(mesh):
    in_specs = (
        P(("grp", "seq"), None),
        P(("grp", "seq"), None),
        P(("grp", "seq"), None),
        P("seq", None),
        P(),
    )
    out_specs = P(("grp", "seq"), None)
    return jax.shard_map(local, mesh=mesh, in_specs=in_specs, out_specs=out_specs, check_vma=False)
```

```python
import functools

import jax
import jax.numpy as jnp
from jax import lax
from jax.experimental import pallas as pl
from jax.experimental.pallas import tpu as pltpu
from jax.sharding import PartitionSpec as P

LANES = 128
COARSE = 16
FINE = 8
CHUNK = 16
TOGETHER = 4


def kernel(
    devices,
    in_gate_hbm,
    values_hbm,
    out_gate_hbm,
    taps_hbm,
    skip_gain_hbm,
    mixed,
    in_gate,
    values,
    out_gate,
    taps,
    skip_gain,
    sent,
    held,
    block,
    turned,
    back,
    conv,
    send_sem,
    recv_sem,
    back_send_sem,
    back_recv_sem,
    load_sem,
):
    loads = [
        pltpu.make_async_copy(source, target, load_sem.at[at])
        for at, (source, target) in enumerate(
            [
                (taps_hbm, taps),
                (in_gate_hbm, in_gate),
                (values_hbm, values),
                (out_gate_hbm, out_gate),
                (skip_gain_hbm, skip_gain),
            ]
        )
    ]
    for load in loads:
        load.start()
    own, channels = in_gate.shape
    share = channels // devices
    chunks = share // CHUNK
    per_owner = own // LANES
    count = per_owner * devices
    width = FINE * count
    me = lax.axis_index("seq")

    barrier = pltpu.get_barrier_semaphore()
    for step in range(1, devices):
        peer = lax.rem(me + step, devices)
        pl.semaphore_signal(
            barrier, inc=1, device_id={"seq": peer}, device_id_type=pl.DeviceIdType.MESH
        )

    flip = (
        lax.broadcasted_iota(jnp.int32, (own, own), 0)
        + lax.broadcasted_iota(jnp.int32, (own, own), 1)
        == own - 1
    )
    flip = flip.astype(jnp.float32).astype(jnp.bfloat16)
    loads[0].wait()
    taps_turned = taps[...].astype(jnp.float32).T.astype(jnp.bfloat16)
    taps_turned = jnp.dot(taps_turned, flip, preferred_element_type=jnp.float32)
    loads[1].wait()
    loads[2].wait()
    gated = in_gate[...].astype(jnp.float32) * values[...].astype(jnp.float32)
    gated = gated.T
    for u in range(per_owner):
        sent[0, u] = gated[:, u * LANES : (u + 1) * LANES]
        sent[1, u] = taps_turned[:, u * LANES : (u + 1) * LANES]

    pl.semaphore_wait(barrier, devices - 1)

    def rows_of(device, chunk):
        return pl.ds(pl.multiple_of(device * share + chunk * CHUNK, CHUNK), CHUNK)

    def forward(step, chunk):
        peer = lax.rem(me + step, devices)
        return pltpu.make_async_remote_copy(
            src_ref=sent.at[:, :, rows_of(peer, chunk), :],
            dst_ref=held.at[me, :, :, pl.ds(chunk * CHUNK, CHUNK), :],
            send_sem=send_sem.at[step, chunk],
            recv_sem=recv_sem.at[step, chunk],
            device_id={"seq": peer},
            device_id_type=pl.DeviceIdType.MESH,
        )

    def backward(step, chunk):
        peer = lax.rem(me + step, devices)
        return pltpu.make_async_remote_copy(
            src_ref=turned.at[chunk, owner_rows(peer), :],
            dst_ref=back.at[me * chunks + chunk],
            send_sem=back_send_sem.at[step, chunk],
            recv_sem=back_recv_sem.at[step, chunk],
            device_id={"seq": peer},
            device_id_type=pl.DeviceIdType.MESH,
        )

    def owner_rows(device):
        start = FINE * per_owner * (devices - 1 - device)
        return pl.ds(pl.multiple_of(start, FINE * per_owner), FINE * per_owner)

    for chunk in range(chunks):
        for step in range(1, devices):
            forward(step, chunk).start()
    for chunk in range(chunks):
        rows = slice(chunk * CHUNK, (chunk + 1) * CHUNK)
        held[me, :, :, rows, :] = sent[:, :, rows_of(me, chunk), :]

    coarse_row = lax.broadcasted_iota(jnp.int32, (COARSE, LANES), 0)
    coarse_lane = lax.broadcasted_iota(jnp.int32, (COARSE, LANES), 1)
    coarse_mask = coarse_lane >= FINE * coarse_row
    fine_row = lax.broadcasted_iota(jnp.int32, (FINE, LANES), 0)
    fine_lane = lax.broadcasted_iota(jnp.int32, (FINE, LANES), 1)
    fine_mask = fine_lane + (FINE - 1) - fine_row < LANES
    wide_lane = lax.broadcasted_iota(jnp.int32, (COARSE, width), 1)

    def convolve(chunk, turn, carry):
        for lane in range(TOGETHER):
            convolve_one(chunk, turn * TOGETHER + lane)
        return carry

    def convolve_one(chunk, at):
        row = pl.ds(chunk * CHUNK + at, 1)
        pieces = []
        before = jnp.zeros((COARSE, LANES), jnp.float32)
        for m in range(count):
            line = held[m // per_owner, 0, m % per_owner, row, :]
            rolled = pltpu.roll(
                jnp.broadcast_to(line, (COARSE, LANES)), 0, 1, stride=FINE, stride_axis=0
            )
            shifted = jnp.where(coarse_mask, rolled, before)
            before = rolled
            high = shifted.astype(jnp.bfloat16)
            low = (shifted - high.astype(jnp.float32)).astype(jnp.bfloat16)
            pieces.append(jnp.concatenate([high, low], axis=1))
        signal = jnp.concatenate(pieces, axis=0)
        pieces = []
        after = jnp.zeros((FINE, LANES), jnp.float32)
        for b in range(count - 1, -1, -1):
            line = held[devices - 1 - b // per_owner, 1, b % per_owner, row, :]
            rolled = pltpu.roll(
                jnp.broadcast_to(line, (FINE, LANES)),
                LANES - FINE + 1,
                1,
                stride=1,
                stride_axis=0,
            )
            pieces.append(jnp.where(fine_mask, rolled, after))
            after = rolled
        filters = jnp.concatenate(pieces[::-1], axis=0).astype(jnp.bfloat16)
        filters = jnp.concatenate([filters, filters], axis=1)
        product = lax.dot_general(
            signal, filters, (((1,), (1,)), ((), ())), preferred_element_type=jnp.float32
        )
        total = product[0:COARSE]
        for m in range(1, count):
            part = product[m * COARSE : (m + 1) * COARSE]
            part = jnp.where(wide_lane >= FINE * m, part, 0.0)
            total = total + pltpu.roll(part, width - FINE * m, 1)
        for group in range(width // LANES):
            block[group, pl.ds(at, COARSE, stride=CHUNK), :] = total[
                :, group * LANES : (group + 1) * LANES
            ]

    for chunk in range(chunks):
        for step in range(1, devices):
            forward(step, chunk).wait_recv()
        lax.fori_loop(0, CHUNK // TOGETHER, functools.partial(convolve, chunk), 0)
        for group in range(width // LANES):
            turned[chunk, group * LANES : (group + 1) * LANES, :] = block[group].T
        for step in range(1, devices):
            backward(step, chunk).start()
        back[me * chunks + chunk] = turned[chunk, owner_rows(me), :]

    for chunk in range(chunks):
        for step in range(1, devices):
            forward(step, chunk).wait_send()
            backward(step, chunk).wait_send()
            backward(step, chunk).wait_recv()

    loads[3].wait()
    loads[4].wait()
    parts = LANES // CHUNK

    def place(group, carry):
        for a in range(COARSE):
            lanes = pl.ds(a * CHUNK, CHUNK)
            merged = jnp.concatenate(
                [back[group * parts + part, :, lanes] for part in range(parts)], axis=1
            )
            for u in range(per_owner):
                start = LANES * (per_owner - 1 - u) + FINE * (COARSE - 1 - a)
                conv[group, start : start + FINE, :] = merged[u * FINE : (u + 1) * FINE]
        return carry

    lax.fori_loop(0, channels // LANES, place, 0)
    for group in range(channels // LANES):
        lanes = slice(group * LANES, (group + 1) * LANES)
        gated = in_gate[:, lanes].astype(jnp.float32) * values[:, lanes].astype(jnp.float32)
        total = conv[group] + skip_gain[:, lanes] * gated
        mixed[:, lanes] = (out_gate[:, lanes].astype(jnp.float32) * total).astype(jnp.bfloat16)


def local(in_gate, values, out_gate, filter_taps, skip_gain):
    own, channels = in_gate.shape
    devices = lax.axis_size("seq")
    share = channels // devices
    chunks = share // CHUNK
    width = FINE * (own // LANES) * devices
    owned = FINE * (own // LANES)
    return pl.pallas_call(
        functools.partial(kernel, devices),
        out_shape=jax.ShapeDtypeStruct((own, channels), jnp.bfloat16),
        in_specs=[pl.BlockSpec(memory_space=pl.ANY)] * 5,
        out_specs=pl.BlockSpec(memory_space=pltpu.VMEM),
        scratch_shapes=[
            pltpu.VMEM((own, channels), jnp.bfloat16),
            pltpu.VMEM((own, channels), jnp.bfloat16),
            pltpu.VMEM((own, channels), jnp.bfloat16),
            pltpu.VMEM((own, channels), jnp.bfloat16),
            pltpu.VMEM((1, channels), jnp.float32),
            pltpu.VMEM((2, own // LANES, channels, LANES), jnp.float32),
            pltpu.VMEM((devices, 2, own // LANES, share, LANES), jnp.float32),
            pltpu.VMEM((width // LANES, COARSE * CHUNK, LANES), jnp.float32),
            pltpu.VMEM((chunks, width, COARSE * CHUNK), jnp.float32),
            pltpu.VMEM((devices * chunks, owned, COARSE * CHUNK), jnp.float32),
            pltpu.VMEM((channels // LANES, own, LANES), jnp.float32),
            pltpu.SemaphoreType.DMA((devices, chunks)),
            pltpu.SemaphoreType.DMA((devices, chunks)),
            pltpu.SemaphoreType.DMA((devices, chunks)),
            pltpu.SemaphoreType.DMA((devices, chunks)),
            pltpu.SemaphoreType.DMA((5,)),
        ],
        compiler_params=pltpu.CompilerParams(
            collective_id=0, has_side_effects=True, vmem_limit_bytes=60 * 1024 * 1024
        ),
    )(in_gate, values, out_gate, filter_taps, skip_gain.reshape(1, channels))


def solution(mesh):
    in_specs = (
        P(("grp", "seq"), None),
        P(("grp", "seq"), None),
        P(("grp", "seq"), None),
        P("seq", None),
        P(),
    )
    out_specs = P(("grp", "seq"), None)
    return jax.shard_map(local, mesh=mesh, in_specs=in_specs, out_specs=out_specs, check_vma=False)
```

```python
import functools

import jax
import jax.numpy as jnp
from jax import lax
from jax.experimental import pallas as pl
from jax.experimental.pallas import tpu as pltpu
from jax.sharding import PartitionSpec as P

LANES = 128
COARSE = 16
FINE = 8
CHUNK = 16
TOGETHER = 4


def kernel(
    devices,
    groups,
    in_gate_hbm,
    values_hbm,
    taps_hbm,
    result,
    in_gate,
    values,
    taps,
    sent,
    signals,
    filters_held,
    block,
    turned,
    back,
    signal_send,
    signal_recv,
    filter_send,
    filter_recv,
    spread_send,
    spread_recv,
    back_send,
    back_recv,
    load_sem,
):
    loads = [
        pltpu.make_async_copy(source, target, load_sem.at[at])
        for at, (source, target) in enumerate(
            [
                (taps_hbm, taps),
                (in_gate_hbm, in_gate),
                (values_hbm, values),
            ]
        )
    ]
    for load in loads:
        load.start()
    own, channels = in_gate.shape
    share = channels // devices
    chunks = share // CHUNK
    per_owner = own // LANES
    count = per_owner * devices
    width = FINE * count
    me = lax.axis_index("seq")
    mine = lax.axis_index("grp")
    shared = chunks == groups and groups % 2 == 0
    pairs = max(groups // 2, 1)

    def group_at(turn, sign):
        if not shared:
            return turn
        pair = lax.rem(lax.div(mine, 2) + sign * (turn // 2) + pairs, pairs)
        return 2 * pair + lax.rem(lax.rem(mine, 2) + turn % 2, 2)

    barrier = pltpu.get_barrier_semaphore()
    for step in range(1, devices):
        peer = lax.rem(me + step, devices)
        pl.semaphore_signal(
            barrier, inc=1, device_id={"seq": peer}, device_id_type=pl.DeviceIdType.MESH
        )
    greeted = devices - 1
    if shared:
        for turn in range(1, groups):
            pl.semaphore_signal(
                barrier,
                inc=1,
                device_id={"grp": group_at(turn, 1)},
                device_id_type=pl.DeviceIdType.MESH,
            )
        greeted += groups - 1

    flip = (
        lax.broadcasted_iota(jnp.int32, (own, own), 0)
        + lax.broadcasted_iota(jnp.int32, (own, own), 1)
        == own - 1
    )
    flip = flip.astype(jnp.float32).astype(jnp.bfloat16)
    loads[0].wait()
    taps_turned = taps[...].astype(jnp.float32).T.astype(jnp.bfloat16)
    taps_turned = jnp.dot(taps_turned, flip, preferred_element_type=jnp.float32)
    loads[1].wait()
    loads[2].wait()
    gated = in_gate[...].astype(jnp.float32) * values[...].astype(jnp.float32)
    gated = gated.T
    for u in range(per_owner):
        sent[0, u] = gated[:, u * LANES : (u + 1) * LANES]
        sent[1, u] = taps_turned[:, u * LANES : (u + 1) * LANES]

    pl.semaphore_wait(barrier, greeted)

    def rows_of(device, chunk):
        return pl.ds(pl.multiple_of(device * share + chunk * CHUNK, CHUNK), CHUNK)

    def forward(which, step, turn):
        peer = lax.rem(me + step, devices)
        chunk = group_at(turn, 1)
        return pltpu.make_async_remote_copy(
            src_ref=sent.at[which, :, rows_of(peer, chunk), :],
            dst_ref=(signals, filters_held)[which].at[me, :, rows_of(0, chunk), :],
            send_sem=(signal_send, filter_send)[which].at[step, turn],
            recv_sem=(signal_recv, filter_recv)[which].at[step, turn],
            device_id={"seq": peer},
            device_id_type=pl.DeviceIdType.MESH,
        )

    def spread(turn):
        region = filters_held.at[:, :, rows_of(0, group_at(0, 1)), :]
        return pltpu.make_async_remote_copy(
            src_ref=region,
            dst_ref=region,
            send_sem=spread_send.at[turn],
            recv_sem=spread_recv.at[turn],
            device_id={"grp": group_at(turn, -1)},
            device_id_type=pl.DeviceIdType.MESH,
        )

    def owner_rows(device):
        start = FINE * per_owner * (devices - 1 - device)
        return pl.ds(pl.multiple_of(start, FINE * per_owner), FINE * per_owner)

    def backward(step, turn):
        peer = lax.rem(me + step, devices)
        return pltpu.make_async_remote_copy(
            src_ref=turned.at[turn, owner_rows(peer), :],
            dst_ref=back.at[me * chunks + group_at(turn, 1)],
            send_sem=back_send.at[step, turn],
            recv_sem=back_recv.at[step, turn],
            device_id={"seq": peer},
            device_id_type=pl.DeviceIdType.MESH,
        )

    filter_turns = 1 if shared else chunks
    for turn in range(chunks):
        for which in (1, 0):
            if which == 0 or turn < filter_turns:
                for step in range(1, devices):
                    forward(which, step, turn).start()
    for turn in range(chunks):
        chunk = group_at(turn, 1)
        signals[me, :, rows_of(0, chunk), :] = sent[0, :, rows_of(me, chunk), :]
        if turn < filter_turns:
            filters_held[me, :, rows_of(0, chunk), :] = sent[1, :, rows_of(me, chunk), :]

    coarse_row = lax.broadcasted_iota(jnp.int32, (COARSE, LANES), 0)
    coarse_lane = lax.broadcasted_iota(jnp.int32, (COARSE, LANES), 1)
    coarse_mask = coarse_lane >= FINE * coarse_row
    fine_row = lax.broadcasted_iota(jnp.int32, (FINE, LANES), 0)
    fine_lane = lax.broadcasted_iota(jnp.int32, (FINE, LANES), 1)
    fine_mask = fine_lane + (FINE - 1) - fine_row < LANES
    wide_lane = lax.broadcasted_iota(jnp.int32, (COARSE, width), 1)

    def convolve(chunk, few, carry):
        for lane in range(TOGETHER):
            convolve_one(chunk, few * TOGETHER + lane)
        return carry

    def convolve_one(chunk, at):
        row = pl.ds(chunk * CHUNK + at, 1)
        pieces = []
        before = jnp.zeros((COARSE, LANES), jnp.float32)
        for m in range(count):
            line = signals[m // per_owner, m % per_owner, row, :]
            rolled = pltpu.roll(
                jnp.broadcast_to(line, (COARSE, LANES)), 0, 1, stride=FINE, stride_axis=0
            )
            shifted = jnp.where(coarse_mask, rolled, before)
            before = rolled
            high = shifted.astype(jnp.bfloat16)
            low = (shifted - high.astype(jnp.float32)).astype(jnp.bfloat16)
            pieces.append(jnp.concatenate([high, low], axis=1))
        signal = jnp.concatenate(pieces, axis=0)
        pieces = []
        after = jnp.zeros((FINE, LANES), jnp.float32)
        for b in range(count - 1, -1, -1):
            line = filters_held[devices - 1 - b // per_owner, b % per_owner, row, :]
            rolled = pltpu.roll(
                jnp.broadcast_to(line, (FINE, LANES)),
                LANES - FINE + 1,
                1,
                stride=1,
                stride_axis=0,
            )
            pieces.append(jnp.where(fine_mask, rolled, after))
            after = rolled
        filters = jnp.concatenate(pieces[::-1], axis=0).astype(jnp.bfloat16)
        filters = jnp.concatenate([filters, filters], axis=1)
        product = lax.dot_general(
            signal, filters, (((1,), (1,)), ((), ())), preferred_element_type=jnp.float32
        )
        total = product[0:COARSE]
        for m in range(1, count):
            part = product[m * COARSE : (m + 1) * COARSE]
            part = jnp.where(wide_lane >= FINE * m, part, 0.0)
            total = total + pltpu.roll(part, width - FINE * m, 1)
        for group in range(width // LANES):
            block[group, pl.ds(at, COARSE, stride=CHUNK), :] = total[
                :, group * LANES : (group + 1) * LANES
            ]

    for turn in range(chunks):
        if turn < filter_turns:
            for step in range(1, devices):
                forward(1, step, turn).wait_recv()
        elif shared:
            spread(turn).wait_recv()
        if shared and turn == 0:
            for other in range(1, groups):
                spread(other).start()
        for step in range(1, devices):
            forward(0, step, turn).wait_recv()
        chunk = group_at(turn, 1)
        lax.fori_loop(0, CHUNK // TOGETHER, functools.partial(convolve, chunk), 0)
        for group in range(width // LANES):
            turned[turn, group * LANES : (group + 1) * LANES, :] = block[group].T
        for step in range(1, devices):
            backward(step, turn).start()
        back[me * chunks + chunk] = turned[turn, owner_rows(me), :]

    for turn in range(chunks):
        for step in range(1, devices):
            backward(step, turn).wait_recv()

    parts = LANES // CHUNK

    def place(group, carry):
        target = pl.ds(pl.multiple_of(group * LANES, LANES), LANES)
        for a in range(COARSE):
            lanes = pl.ds(a * CHUNK, CHUNK)
            merged = jnp.concatenate(
                [back[group * parts + part, :, lanes] for part in range(parts)], axis=1
            )
            for u in range(per_owner):
                start = LANES * (per_owner - 1 - u) + FINE * (COARSE - 1 - a)
                result[start : start + FINE, target] = merged[u * FINE : (u + 1) * FINE]
        return carry

    lax.fori_loop(0, channels // LANES, place, 0)
    for turn in range(chunks):
        for step in range(1, devices):
            forward(0, step, turn).wait_send()
            if turn < filter_turns:
                forward(1, step, turn).wait_send()
            backward(step, turn).wait_send()
    if shared:
        for turn in range(1, groups):
            spread(turn).wait_send()


def local(in_gate, values, out_gate, filter_taps, skip_gain):
    own, channels = in_gate.shape
    devices = lax.axis_size("seq")
    groups = lax.axis_size("grp")
    share = channels // devices
    chunks = share // CHUNK
    width = FINE * (own // LANES) * devices
    owned = FINE * (own // LANES)
    pieces = pltpu.SemaphoreType.DMA((devices, chunks))
    conv = pl.pallas_call(
        functools.partial(kernel, devices, groups),
        out_shape=jax.ShapeDtypeStruct((own, channels), jnp.float32),
        in_specs=[pl.BlockSpec(memory_space=pl.ANY)] * 3,
        out_specs=pl.BlockSpec(memory_space=pltpu.VMEM),
        scratch_shapes=[
            pltpu.VMEM((own, channels), jnp.bfloat16),
            pltpu.VMEM((own, channels), jnp.bfloat16),
            pltpu.VMEM((own, channels), jnp.bfloat16),
            pltpu.VMEM((2, own // LANES, channels, LANES), jnp.float32),
            pltpu.VMEM((devices, own // LANES, share, LANES), jnp.float32),
            pltpu.VMEM((devices, own // LANES, share, LANES), jnp.float32),
            pltpu.VMEM((width // LANES, COARSE * CHUNK, LANES), jnp.float32),
            pltpu.VMEM((chunks, width, COARSE * CHUNK), jnp.float32),
            pltpu.VMEM((devices * chunks, owned, COARSE * CHUNK), jnp.float32),
            pieces,
            pieces,
            pieces,
            pieces,
            pltpu.SemaphoreType.DMA((groups,)),
            pltpu.SemaphoreType.DMA((groups,)),
            pieces,
            pieces,
            pltpu.SemaphoreType.DMA((3,)),
        ],
        compiler_params=pltpu.CompilerParams(
            collective_id=0, has_side_effects=True, vmem_limit_bytes=60 * 1024 * 1024
        ),
    )(in_gate, values, filter_taps)
    gated = in_gate.astype(jnp.float32) * values.astype(jnp.float32)
    total = conv + skip_gain[None, :] * gated
    return (out_gate.astype(jnp.float32) * total).astype(jnp.bfloat16)


def solution(mesh):
    in_specs = (
        P(("grp", "seq"), None),
        P(("grp", "seq"), None),
        P(("grp", "seq"), None),
        P("seq", None),
        P(),
    )
    out_specs = P(("grp", "seq"), None)
    return jax.shard_map(local, mesh=mesh, in_specs=in_specs, out_specs=out_specs, check_vma=False)
```

```python
import functools

import jax
import jax.numpy as jnp
from jax import lax
from jax.experimental import pallas as pl
from jax.experimental.pallas import tpu as pltpu
from jax.sharding import PartitionSpec as P

LANES = 128
COARSE = 16
FINE = 8
CHUNK = 16
TOGETHER = 8


def kernel(
    devices,
    groups,
    in_gate_hbm,
    values_hbm,
    taps_hbm,
    result,
    in_gate,
    values,
    taps,
    sent,
    signals,
    filters_held,
    block,
    turned,
    back,
    signal_send,
    signal_recv,
    filter_send,
    filter_recv,
    spread_send,
    spread_recv,
    back_send,
    back_recv,
    load_sem,
):
    loads = [
        pltpu.make_async_copy(source, target, load_sem.at[at])
        for at, (source, target) in enumerate(
            [
                (in_gate_hbm, in_gate),
                (values_hbm, values),
                (taps_hbm, taps),
            ]
        )
    ]
    for load in loads:
        load.start()
    own, channels = in_gate.shape
    share = channels // devices
    chunks = share // CHUNK
    per_owner = own // LANES
    count = per_owner * devices
    width = FINE * count
    me = lax.axis_index("seq")
    mine = lax.axis_index("grp")
    shared = chunks == groups and groups % 2 == 0
    pairs = max(groups // 2, 1)

    def group_at(turn, sign):
        if not shared:
            return turn
        pair = lax.rem(lax.div(mine, 2) + sign * (turn // 2) + pairs, pairs)
        return 2 * pair + lax.rem(lax.rem(mine, 2) + turn % 2, 2)

    barrier = pltpu.get_barrier_semaphore()
    for step in range(1, devices):
        peer = lax.rem(me + step, devices)
        pl.semaphore_signal(
            barrier, inc=1, device_id={"seq": peer}, device_id_type=pl.DeviceIdType.MESH
        )
    greeted = devices - 1
    if shared:
        for turn in range(1, groups):
            pl.semaphore_signal(
                barrier,
                inc=1,
                device_id={"grp": group_at(turn, 1)},
                device_id_type=pl.DeviceIdType.MESH,
            )
        greeted += groups - 1

    loads[0].wait()
    loads[1].wait()
    gated = in_gate[...].astype(jnp.float32) * values[...].astype(jnp.float32)
    gated = gated.T
    for u in range(per_owner):
        sent[0, u] = gated[:, u * LANES : (u + 1) * LANES]

    pl.semaphore_wait(barrier, greeted)

    def rows_of(device, chunk):
        return pl.ds(pl.multiple_of(device * share + chunk * CHUNK, CHUNK), CHUNK)

    def forward(which, step, turn):
        peer = lax.rem(me + step, devices)
        chunk = group_at(turn, 1)
        return pltpu.make_async_remote_copy(
            src_ref=sent.at[which, :, rows_of(peer, chunk), :],
            dst_ref=(signals, filters_held)[which].at[me, :, rows_of(0, chunk), :],
            send_sem=(signal_send, filter_send)[which].at[step, turn],
            recv_sem=(signal_recv, filter_recv)[which].at[step, turn],
            device_id={"seq": peer},
            device_id_type=pl.DeviceIdType.MESH,
        )

    def spread(turn):
        region = filters_held.at[:, :, rows_of(0, group_at(0, 1)), :]
        return pltpu.make_async_remote_copy(
            src_ref=region,
            dst_ref=region,
            send_sem=spread_send.at[turn],
            recv_sem=spread_recv.at[turn],
            device_id={"grp": group_at(turn, -1)},
            device_id_type=pl.DeviceIdType.MESH,
        )

    def owner_rows(device):
        start = FINE * per_owner * (devices - 1 - device)
        return pl.ds(pl.multiple_of(start, FINE * per_owner), FINE * per_owner)

    def backward(step, turn):
        peer = lax.rem(me + step, devices)
        return pltpu.make_async_remote_copy(
            src_ref=turned.at[turn, owner_rows(peer), :],
            dst_ref=back.at[me * chunks + group_at(turn, 1)],
            send_sem=back_send.at[step, turn],
            recv_sem=back_recv.at[step, turn],
            device_id={"seq": peer},
            device_id_type=pl.DeviceIdType.MESH,
        )

    for step in range(1, devices):
        forward(0, step, 0).start()

    flip = (
        lax.broadcasted_iota(jnp.int32, (own, own), 0)
        + lax.broadcasted_iota(jnp.int32, (own, own), 1)
        == own - 1
    )
    flip = flip.astype(jnp.float32).astype(jnp.bfloat16)
    loads[2].wait()
    taps_turned = taps[...].astype(jnp.float32).T.astype(jnp.bfloat16)
    taps_turned = jnp.dot(taps_turned, flip, preferred_element_type=jnp.float32)
    for u in range(per_owner):
        sent[1, u] = taps_turned[:, u * LANES : (u + 1) * LANES]

    filter_turns = 1 if shared else chunks
    for turn in range(chunks):
        for which in (1, 0):
            if (which == 0 and turn > 0) or (which == 1 and turn < filter_turns):
                for step in range(1, devices):
                    forward(which, step, turn).start()
    for turn in range(chunks):
        chunk = group_at(turn, 1)
        signals[me, :, rows_of(0, chunk), :] = sent[0, :, rows_of(me, chunk), :]
        if turn < filter_turns:
            filters_held[me, :, rows_of(0, chunk), :] = sent[1, :, rows_of(me, chunk), :]

    coarse_row = lax.broadcasted_iota(jnp.int32, (COARSE, LANES), 0)
    coarse_lane = lax.broadcasted_iota(jnp.int32, (COARSE, LANES), 1)
    coarse_mask = coarse_lane >= FINE * coarse_row
    fine_row = lax.broadcasted_iota(jnp.int32, (FINE, LANES), 0)
    fine_lane = lax.broadcasted_iota(jnp.int32, (FINE, LANES), 1)
    fine_mask = fine_lane + (FINE - 1) - fine_row < LANES
    wide_lane = lax.broadcasted_iota(jnp.int32, (COARSE, width), 1)

    def convolve(chunk, few, carry):
        for lane in range(TOGETHER):
            convolve_one(chunk, few * TOGETHER + lane)
        return carry

    def convolve_one(chunk, at):
        row = pl.ds(chunk * CHUNK + at, 1)
        pieces = []
        before = jnp.zeros((COARSE, LANES), jnp.float32)
        for m in range(count):
            line = signals[m // per_owner, m % per_owner, row, :]
            rolled = pltpu.roll(
                jnp.broadcast_to(line, (COARSE, LANES)), 0, 1, stride=FINE, stride_axis=0
            )
            shifted = jnp.where(coarse_mask, rolled, before)
            before = rolled
            high = shifted.astype(jnp.bfloat16)
            low = (shifted - high.astype(jnp.float32)).astype(jnp.bfloat16)
            pieces.append(jnp.concatenate([high, low], axis=1))
        signal = jnp.concatenate(pieces, axis=0)
        pieces = []
        after = jnp.zeros((FINE, LANES), jnp.float32)
        for b in range(count - 1, -1, -1):
            line = filters_held[devices - 1 - b // per_owner, b % per_owner, row, :]
            rolled = pltpu.roll(
                jnp.broadcast_to(line, (FINE, LANES)),
                LANES - FINE + 1,
                1,
                stride=1,
                stride_axis=0,
            )
            pieces.append(jnp.where(fine_mask, rolled, after))
            after = rolled
        filters = jnp.concatenate(pieces[::-1], axis=0).astype(jnp.bfloat16)
        filters = jnp.concatenate([filters, filters], axis=1)
        product = lax.dot_general(
            signal, filters, (((1,), (1,)), ((), ())), preferred_element_type=jnp.float32
        )
        total = product[0:COARSE]
        for m in range(1, count):
            part = product[m * COARSE : (m + 1) * COARSE]
            part = jnp.where(wide_lane >= FINE * m, part, 0.0)
            total = total + pltpu.roll(part, width - FINE * m, 1)
        for group in range(width // LANES):
            block[group, pl.ds(at, COARSE, stride=CHUNK), :] = total[
                :, group * LANES : (group + 1) * LANES
            ]

    for turn in range(chunks):
        if turn < filter_turns:
            for step in range(1, devices):
                forward(1, step, turn).wait_recv()
        elif shared:
            spread(turn).wait_recv()
        if shared and turn == 0:
            for other in range(1, groups):
                spread(other).start()
        for step in range(1, devices):
            forward(0, step, turn).wait_recv()
        chunk = group_at(turn, 1)
        lax.fori_loop(0, CHUNK // TOGETHER, functools.partial(convolve, chunk), 0)
        for group in range(width // LANES):
            turned[turn, group * LANES : (group + 1) * LANES, :] = block[group].T
        for step in range(1, devices):
            backward(step, turn).start()
        back[me * chunks + chunk] = turned[turn, owner_rows(me), :]

    for turn in range(chunks):
        for step in range(1, devices):
            backward(step, turn).wait_recv()

    parts = LANES // CHUNK

    def place(group, carry):
        target = pl.ds(pl.multiple_of(group * LANES, LANES), LANES)
        for a in range(COARSE):
            lanes = pl.ds(a * CHUNK, CHUNK)
            merged = jnp.concatenate(
                [back[group * parts + part, :, lanes] for part in range(parts)], axis=1
            )
            for u in range(per_owner):
                start = LANES * (per_owner - 1 - u) + FINE * (COARSE - 1 - a)
                result[start : start + FINE, target] = merged[u * FINE : (u + 1) * FINE]
        return carry

    lax.fori_loop(0, channels // LANES, place, 0)
    for turn in range(chunks):
        for step in range(1, devices):
            forward(0, step, turn).wait_send()
            if turn < filter_turns:
                forward(1, step, turn).wait_send()
            backward(step, turn).wait_send()
    if shared:
        for turn in range(1, groups):
            spread(turn).wait_send()


def local(in_gate, values, out_gate, filter_taps, skip_gain):
    own, channels = in_gate.shape
    devices = lax.axis_size("seq")
    groups = lax.axis_size("grp")
    share = channels // devices
    chunks = share // CHUNK
    width = FINE * (own // LANES) * devices
    owned = FINE * (own // LANES)
    pieces = pltpu.SemaphoreType.DMA((devices, chunks))
    conv = pl.pallas_call(
        functools.partial(kernel, devices, groups),
        out_shape=jax.ShapeDtypeStruct((own, channels), jnp.float32),
        in_specs=[pl.BlockSpec(memory_space=pl.ANY)] * 3,
        out_specs=pl.BlockSpec(memory_space=pltpu.VMEM),
        scratch_shapes=[
            pltpu.VMEM((own, channels), jnp.bfloat16),
            pltpu.VMEM((own, channels), jnp.bfloat16),
            pltpu.VMEM((own, channels), jnp.bfloat16),
            pltpu.VMEM((2, own // LANES, channels, LANES), jnp.float32),
            pltpu.VMEM((devices, own // LANES, share, LANES), jnp.float32),
            pltpu.VMEM((devices, own // LANES, share, LANES), jnp.float32),
            pltpu.VMEM((width // LANES, COARSE * CHUNK, LANES), jnp.float32),
            pltpu.VMEM((chunks, width, COARSE * CHUNK), jnp.float32),
            pltpu.VMEM((devices * chunks, owned, COARSE * CHUNK), jnp.float32),
            pieces,
            pieces,
            pieces,
            pieces,
            pltpu.SemaphoreType.DMA((groups,)),
            pltpu.SemaphoreType.DMA((groups,)),
            pieces,
            pieces,
            pltpu.SemaphoreType.DMA((3,)),
        ],
        compiler_params=pltpu.CompilerParams(
            collective_id=0, has_side_effects=True, vmem_limit_bytes=60 * 1024 * 1024
        ),
    )(in_gate, values, filter_taps)
    gated = in_gate.astype(jnp.float32) * values.astype(jnp.float32)
    total = conv + skip_gain[None, :] * gated
    return (out_gate.astype(jnp.float32) * total).astype(jnp.bfloat16)


def solution(mesh):
    in_specs = (
        P(("grp", "seq"), None),
        P(("grp", "seq"), None),
        P(("grp", "seq"), None),
        P("seq", None),
        P(),
    )
    out_specs = P(("grp", "seq"), None)
    return jax.shard_map(local, mesh=mesh, in_specs=in_specs, out_specs=out_specs, check_vma=False)
```

```python
import functools

import jax
import jax.numpy as jnp
from jax import lax
from jax.experimental import pallas as pl
from jax.experimental.pallas import tpu as pltpu
from jax.sharding import PartitionSpec as P

LANES = 128
COARSE = 16
FINE = 8
CHUNK = 16
TOGETHER = 4


def kernel(
    devices,
    groups,
    in_gate_hbm,
    values_hbm,
    taps_hbm,
    result,
    in_gate,
    values,
    taps,
    sent,
    signals,
    filters_held,
    block,
    turned,
    back,
    signal_send,
    signal_recv,
    filter_send,
    filter_recv,
    spread_send,
    spread_recv,
    back_send,
    back_recv,
    load_sem,
    placed,
    placed_sem,
):
    loads = [
        pltpu.make_async_copy(source, target, load_sem.at[at])
        for at, (source, target) in enumerate(
            [
                (taps_hbm, taps),
                (in_gate_hbm, in_gate),
                (values_hbm, values),
            ]
        )
    ]
    for load in loads:
        load.start()
    own, channels = in_gate.shape
    share = channels // devices
    chunks = share // CHUNK
    per_owner = own // LANES
    count = per_owner * devices
    width = FINE * count
    me = lax.axis_index("seq")
    mine = lax.axis_index("grp")
    half = devices // 2
    order = [step for at in range(half) for step in (half + at, 1 + at)][: devices - 1]

    def partner(step):
        peer, bit = me * 0, 1
        while bit < devices:
            own_bit = lax.rem(lax.div(me, bit), 2)
            peer = peer + bit * (1 - own_bit if step & bit else own_bit)
            bit *= 2
        return peer

    shared = chunks == groups and groups % 2 == 0
    pairs = max(groups // 2, 1)

    def group_at(turn, sign):
        if not shared:
            return turn
        pair = lax.rem(lax.div(mine, 2) + sign * (turn // 2) + pairs, pairs)
        return 2 * pair + lax.rem(lax.rem(mine, 2) + turn % 2, 2)

    barrier = pltpu.get_barrier_semaphore()
    for step in order:
        peer = partner(step)
        pl.semaphore_signal(
            barrier, inc=1, device_id={"seq": peer}, device_id_type=pl.DeviceIdType.MESH
        )
    greeted = devices - 1
    if shared:
        for turn in range(1, groups):
            pl.semaphore_signal(
                barrier,
                inc=1,
                device_id={"grp": group_at(turn, 1)},
                device_id_type=pl.DeviceIdType.MESH,
            )
        greeted += groups - 1

    flip = (
        lax.broadcasted_iota(jnp.int32, (own, own), 0)
        + lax.broadcasted_iota(jnp.int32, (own, own), 1)
        == own - 1
    )
    flip = flip.astype(jnp.float32).astype(jnp.bfloat16)
    loads[0].wait()
    taps_turned = taps[...].astype(jnp.float32).T.astype(jnp.bfloat16)
    taps_turned = jnp.dot(taps_turned, flip, preferred_element_type=jnp.float32)
    loads[1].wait()
    loads[2].wait()
    gated = in_gate[...].astype(jnp.float32) * values[...].astype(jnp.float32)
    gated = gated.T
    for u in range(per_owner):
        sent[0, u] = gated[:, u * LANES : (u + 1) * LANES]
        sent[1, u] = taps_turned[:, u * LANES : (u + 1) * LANES]

    pl.semaphore_wait(barrier, greeted)

    def rows_of(device, chunk):
        return pl.ds(pl.multiple_of(device * share + chunk * CHUNK, CHUNK), CHUNK)

    def forward(which, step, turn):
        peer = partner(step)
        chunk = group_at(turn, 1)
        return pltpu.make_async_remote_copy(
            src_ref=sent.at[which, :, rows_of(peer, chunk), :],
            dst_ref=(signals, filters_held)[which].at[me, :, rows_of(0, chunk), :],
            send_sem=(signal_send, filter_send)[which].at[step, turn],
            recv_sem=(signal_recv, filter_recv)[which].at[step, turn],
            device_id={"seq": peer},
            device_id_type=pl.DeviceIdType.MESH,
        )

    def spread(turn):
        region = filters_held.at[:, :, rows_of(0, group_at(0, 1)), :]
        return pltpu.make_async_remote_copy(
            src_ref=region,
            dst_ref=region,
            send_sem=spread_send.at[turn],
            recv_sem=spread_recv.at[turn],
            device_id={"grp": group_at(turn, -1)},
            device_id_type=pl.DeviceIdType.MESH,
        )

    def owner_rows(device):
        start = FINE * per_owner * (devices - 1 - device)
        return pl.ds(pl.multiple_of(start, FINE * per_owner), FINE * per_owner)

    def backward(step, turn):
        peer = partner(step)
        return pltpu.make_async_remote_copy(
            src_ref=turned.at[turn, owner_rows(peer), :],
            dst_ref=back.at[me * chunks + group_at(turn, 1)],
            send_sem=back_send.at[step, turn],
            recv_sem=back_recv.at[step, turn],
            device_id={"seq": peer},
            device_id_type=pl.DeviceIdType.MESH,
        )

    filter_turns = 1 if shared else chunks
    for turn in range(chunks):
        for which in (1, 0):
            if which == 0 or turn < filter_turns:
                for step in order:
                    forward(which, step, turn).start()
    for turn in range(chunks):
        chunk = group_at(turn, 1)
        signals[me, :, rows_of(0, chunk), :] = sent[0, :, rows_of(me, chunk), :]
        if turn < filter_turns:
            filters_held[me, :, rows_of(0, chunk), :] = sent[1, :, rows_of(me, chunk), :]

    coarse_row = lax.broadcasted_iota(jnp.int32, (COARSE, LANES), 0)
    coarse_lane = lax.broadcasted_iota(jnp.int32, (COARSE, LANES), 1)
    coarse_mask = coarse_lane >= FINE * coarse_row
    fine_row = lax.broadcasted_iota(jnp.int32, (FINE, LANES), 0)
    fine_lane = lax.broadcasted_iota(jnp.int32, (FINE, LANES), 1)
    fine_mask = fine_lane + (FINE - 1) - fine_row < LANES
    wide_lane = lax.broadcasted_iota(jnp.int32, (COARSE, width), 1)

    def convolve(chunk, few, carry):
        for lane in range(TOGETHER):
            convolve_one(chunk, few * TOGETHER + lane)
        return carry

    def convolve_one(chunk, at):
        row = pl.ds(chunk * CHUNK + at, 1)
        pieces = []
        before = jnp.zeros((COARSE, LANES), jnp.float32)
        for m in range(count):
            line = signals[m // per_owner, m % per_owner, row, :]
            rolled = pltpu.roll(
                jnp.broadcast_to(line, (COARSE, LANES)), 0, 1, stride=FINE, stride_axis=0
            )
            shifted = jnp.where(coarse_mask, rolled, before)
            before = rolled
            high = shifted.astype(jnp.bfloat16)
            low = (shifted - high.astype(jnp.float32)).astype(jnp.bfloat16)
            pieces.append(jnp.concatenate([high, low], axis=1))
        signal = jnp.concatenate(pieces, axis=0)
        pieces = []
        after = jnp.zeros((FINE, LANES), jnp.float32)
        for b in range(count - 1, -1, -1):
            line = filters_held[devices - 1 - b // per_owner, b % per_owner, row, :]
            rolled = pltpu.roll(
                jnp.broadcast_to(line, (FINE, LANES)),
                LANES - FINE + 1,
                1,
                stride=1,
                stride_axis=0,
            )
            pieces.append(jnp.where(fine_mask, rolled, after))
            after = rolled
        filters = jnp.concatenate(pieces[::-1], axis=0).astype(jnp.bfloat16)
        filters = jnp.concatenate([filters, filters], axis=1)
        product = lax.dot_general(
            signal, filters, (((1,), (1,)), ((), ())), preferred_element_type=jnp.float32
        )
        total = product[0:COARSE]
        for m in range(1, count):
            part = product[m * COARSE : (m + 1) * COARSE]
            part = jnp.where(wide_lane >= FINE * m, part, 0.0)
            total = total + pltpu.roll(part, width - FINE * m, 1)
        for group in range(width // LANES):
            block[group, pl.ds(at, COARSE, stride=CHUNK), :] = total[
                :, group * LANES : (group + 1) * LANES
            ]

    for turn in range(chunks):
        if turn < filter_turns:
            for step in order:
                forward(1, step, turn).wait_recv()
        elif shared:
            spread(turn).wait_recv()
        if shared and turn == 0:
            for other in range(1, groups):
                spread(other).start()
        for step in order:
            forward(0, step, turn).wait_recv()
        chunk = group_at(turn, 1)
        lax.fori_loop(0, CHUNK // TOGETHER, functools.partial(convolve, chunk), 0)
        for group in range(width // LANES):
            turned[turn, group * LANES : (group + 1) * LANES, :] = block[group].T
        for step in order:
            backward(step, turn).start()
        back[me * chunks + chunk] = turned[turn, owner_rows(me), :]

    for turn in range(chunks):
        for step in order:
            backward(step, turn).wait_recv()

    parts = LANES // CHUNK

    def store(group):
        target = pl.ds(pl.multiple_of(group * LANES, LANES), LANES)
        return pltpu.make_async_copy(
            placed.at[group], result.at[:, target], placed_sem.at[group]
        )

    def place(group, carry):
        for a in range(COARSE):
            lanes = pl.ds(a * CHUNK, CHUNK)
            merged = jnp.concatenate(
                [back[group * parts + part, :, lanes] for part in range(parts)], axis=1
            )
            for u in range(per_owner):
                start = LANES * (per_owner - 1 - u) + FINE * (COARSE - 1 - a)
                placed[group, start : start + FINE, :] = merged[u * FINE : (u + 1) * FINE]
        store(group).start()
        return carry

    lax.fori_loop(0, channels // LANES, place, 0)
    for turn in range(chunks):
        for step in order:
            forward(0, step, turn).wait_send()
            if turn < filter_turns:
                forward(1, step, turn).wait_send()
            backward(step, turn).wait_send()
    if shared:
        for turn in range(1, groups):
            spread(turn).wait_send()
    for group in range(channels // LANES):
        store(group).wait()


def local(in_gate, values, out_gate, filter_taps, skip_gain):
    own, channels = in_gate.shape
    devices = lax.axis_size("seq")
    groups = lax.axis_size("grp")
    share = channels // devices
    chunks = share // CHUNK
    width = FINE * (own // LANES) * devices
    owned = FINE * (own // LANES)
    pieces = pltpu.SemaphoreType.DMA((devices, chunks))
    conv = pl.pallas_call(
        functools.partial(kernel, devices, groups),
        out_shape=jax.ShapeDtypeStruct((own, channels), jnp.float32),
        in_specs=[pl.BlockSpec(memory_space=pl.ANY)] * 3,
        out_specs=pl.BlockSpec(memory_space=pl.ANY),
        scratch_shapes=[
            pltpu.VMEM((own, channels), jnp.bfloat16),
            pltpu.VMEM((own, channels), jnp.bfloat16),
            pltpu.VMEM((own, channels), jnp.bfloat16),
            pltpu.VMEM((2, own // LANES, channels, LANES), jnp.float32),
            pltpu.VMEM((devices, own // LANES, share, LANES), jnp.float32),
            pltpu.VMEM((devices, own // LANES, share, LANES), jnp.float32),
            pltpu.VMEM((width // LANES, COARSE * CHUNK, LANES), jnp.float32),
            pltpu.VMEM((chunks, width, COARSE * CHUNK), jnp.float32),
            pltpu.VMEM((devices * chunks, owned, COARSE * CHUNK), jnp.float32),
            pieces,
            pieces,
            pieces,
            pieces,
            pltpu.SemaphoreType.DMA((groups,)),
            pltpu.SemaphoreType.DMA((groups,)),
            pieces,
            pieces,
            pltpu.SemaphoreType.DMA((3,)),
            pltpu.VMEM((channels // LANES, own, LANES), jnp.float32),
            pltpu.SemaphoreType.DMA((channels // LANES,)),
        ],
        compiler_params=pltpu.CompilerParams(
            collective_id=0, has_side_effects=True, vmem_limit_bytes=60 * 1024 * 1024
        ),
    )(in_gate, values, filter_taps)
    gated = in_gate.astype(jnp.float32) * values.astype(jnp.float32)
    total = conv + skip_gain[None, :] * gated
    return (out_gate.astype(jnp.float32) * total).astype(jnp.bfloat16)


def solution(mesh):
    in_specs = (
        P(("grp", "seq"), None),
        P(("grp", "seq"), None),
        P(("grp", "seq"), None),
        P("seq", None),
        P(),
    )
    out_specs = P(("grp", "seq"), None)
    return jax.shard_map(local, mesh=mesh, in_specs=in_specs, out_specs=out_specs, check_vma=False)
```

```python
import functools

import jax
import jax.numpy as jnp
from jax import lax
from jax.experimental import pallas as pl
from jax.experimental.pallas import tpu as pltpu
from jax.sharding import PartitionSpec as P

LANES = 128
COARSE = 16
FINE = 8
CHUNK = 16
TOGETHER = 4


def kernel(
    devices,
    groups,
    in_gate_hbm,
    values_hbm,
    taps_hbm,
    result,
    in_gate,
    values,
    taps,
    sent,
    signals,
    filters_held,
    block,
    turned,
    back,
    signal_send,
    signal_recv,
    filter_send,
    filter_recv,
    spread_send,
    spread_recv,
    back_send,
    back_recv,
    load_sem,
    placed,
    placed_sem,
):
    loads = [
        pltpu.make_async_copy(source, target, load_sem.at[at])
        for at, (source, target) in enumerate(
            [
                (in_gate_hbm, in_gate),
                (values_hbm, values),
                (taps_hbm, taps),
            ]
        )
    ]
    for load in loads:
        load.start()
    own, channels = in_gate.shape
    share = channels // devices
    chunks = share // CHUNK
    per_owner = own // LANES
    count = per_owner * devices
    width = FINE * count
    me = lax.axis_index("seq")
    mine = lax.axis_index("grp")
    half = devices // 2
    order = [step for at in range(half) for step in (half + at, 1 + at)][: devices - 1]

    def partner(step):
        peer, bit = me * 0, 1
        while bit < devices:
            own_bit = lax.rem(lax.div(me, bit), 2)
            peer = peer + bit * (1 - own_bit if step & bit else own_bit)
            bit *= 2
        return peer

    shared = chunks == groups and groups % 2 == 0
    pairs = max(groups // 2, 1)

    def group_at(turn, sign):
        if not shared:
            return turn
        pair = lax.rem(lax.div(mine, 2) + sign * (turn // 2) + pairs, pairs)
        return 2 * pair + lax.rem(lax.rem(mine, 2) + turn % 2, 2)

    barrier = pltpu.get_barrier_semaphore()
    for step in order:
        peer = partner(step)
        pl.semaphore_signal(
            barrier, inc=1, device_id={"seq": peer}, device_id_type=pl.DeviceIdType.MESH
        )
    greeted = devices - 1
    if shared:
        for turn in range(1, groups):
            pl.semaphore_signal(
                barrier,
                inc=1,
                device_id={"grp": group_at(turn, 1)},
                device_id_type=pl.DeviceIdType.MESH,
            )
        greeted += groups - 1

    reach = devices * CHUNK

    def columns_of(chunk):
        return pl.ds(pl.multiple_of(chunk * reach, LANES), reach)

    def turn_signal(turn):
        columns = columns_of(group_at(turn, 1))
        gated = in_gate[:, columns].astype(jnp.float32) * values[:, columns].astype(jnp.float32)
        gated = gated.T
        for u in range(per_owner):
            sent[0, u, columns, :] = gated[:, u * LANES : (u + 1) * LANES]

    def turn_filter(turn):
        columns = columns_of(group_at(turn, 1))
        flip = (
            lax.broadcasted_iota(jnp.int32, (own, own), 0)
            + lax.broadcasted_iota(jnp.int32, (own, own), 1)
            == own - 1
        )
        flip = flip.astype(jnp.float32).astype(jnp.bfloat16)
        turned_taps = taps[:, columns].astype(jnp.float32).T.astype(jnp.bfloat16)
        turned_taps = jnp.dot(turned_taps, flip, preferred_element_type=jnp.float32)
        for u in range(per_owner):
            sent[1, u, columns, :] = turned_taps[:, u * LANES : (u + 1) * LANES]

    loads[0].wait()
    loads[1].wait()
    turn_signal(0)

    pl.semaphore_wait(barrier, greeted)

    def rows_of(device, chunk):
        return pl.ds(pl.multiple_of((chunk * devices + device) * CHUNK, CHUNK), CHUNK)

    def rows_in(chunk):
        return pl.ds(pl.multiple_of(chunk * CHUNK, CHUNK), CHUNK)

    def forward(which, step, turn):
        peer = partner(step)
        chunk = group_at(turn, 1)
        return pltpu.make_async_remote_copy(
            src_ref=sent.at[which, :, rows_of(peer, chunk), :],
            dst_ref=(signals, filters_held)[which].at[me, :, rows_in(chunk), :],
            send_sem=(signal_send, filter_send)[which].at[step, turn],
            recv_sem=(signal_recv, filter_recv)[which].at[step, turn],
            device_id={"seq": peer},
            device_id_type=pl.DeviceIdType.MESH,
        )

    def spread(turn):
        region = filters_held.at[:, :, rows_in(group_at(0, 1)), :]
        return pltpu.make_async_remote_copy(
            src_ref=region,
            dst_ref=region,
            send_sem=spread_send.at[turn],
            recv_sem=spread_recv.at[turn],
            device_id={"grp": group_at(turn, -1)},
            device_id_type=pl.DeviceIdType.MESH,
        )

    def owner_rows(device):
        start = FINE * per_owner * (devices - 1 - device)
        return pl.ds(pl.multiple_of(start, FINE * per_owner), FINE * per_owner)

    def backward(step, turn):
        peer = partner(step)
        return pltpu.make_async_remote_copy(
            src_ref=turned.at[turn, owner_rows(peer), :],
            dst_ref=back.at[group_at(turn, 1) * devices + me],
            send_sem=back_send.at[step, turn],
            recv_sem=back_recv.at[step, turn],
            device_id={"seq": peer},
            device_id_type=pl.DeviceIdType.MESH,
        )

    filter_turns = 1 if shared else chunks
    for turn in range(chunks):
        if turn > 0:
            turn_signal(turn)
        for step in order:
            forward(0, step, turn).start()
        if turn < filter_turns:
            if turn == 0:
                loads[2].wait()
            turn_filter(turn)
            for step in order:
                forward(1, step, turn).start()
    for turn in range(chunks):
        chunk = group_at(turn, 1)
        signals[me, :, rows_in(chunk), :] = sent[0, :, rows_of(me, chunk), :]
        if turn < filter_turns:
            filters_held[me, :, rows_in(chunk), :] = sent[1, :, rows_of(me, chunk), :]

    coarse_row = lax.broadcasted_iota(jnp.int32, (COARSE, LANES), 0)
    coarse_lane = lax.broadcasted_iota(jnp.int32, (COARSE, LANES), 1)
    coarse_mask = coarse_lane >= FINE * coarse_row
    fine_row = lax.broadcasted_iota(jnp.int32, (FINE, LANES), 0)
    fine_lane = lax.broadcasted_iota(jnp.int32, (FINE, LANES), 1)
    fine_mask = fine_lane + (FINE - 1) - fine_row < LANES
    wide_lane = lax.broadcasted_iota(jnp.int32, (COARSE, width), 1)

    def convolve(chunk, few, carry):
        for lane in range(TOGETHER):
            convolve_one(chunk, few * TOGETHER + lane)
        return carry

    def convolve_one(chunk, at):
        row = pl.ds(chunk * CHUNK + at, 1)
        pieces = []
        before = jnp.zeros((COARSE, LANES), jnp.float32)
        for m in range(count):
            line = signals[m // per_owner, m % per_owner, row, :]
            rolled = pltpu.roll(
                jnp.broadcast_to(line, (COARSE, LANES)), 0, 1, stride=FINE, stride_axis=0
            )
            shifted = jnp.where(coarse_mask, rolled, before)
            before = rolled
            high = shifted.astype(jnp.bfloat16)
            low = (shifted - high.astype(jnp.float32)).astype(jnp.bfloat16)
            pieces.append(jnp.concatenate([high, low], axis=1))
        signal = jnp.concatenate(pieces, axis=0)
        pieces = []
        after = jnp.zeros((FINE, LANES), jnp.float32)
        for b in range(count - 1, -1, -1):
            line = filters_held[devices - 1 - b // per_owner, b % per_owner, row, :]
            rolled = pltpu.roll(
                jnp.broadcast_to(line, (FINE, LANES)),
                LANES - FINE + 1,
                1,
                stride=1,
                stride_axis=0,
            )
            pieces.append(jnp.where(fine_mask, rolled, after))
            after = rolled
        filters = jnp.concatenate(pieces[::-1], axis=0).astype(jnp.bfloat16)
        filters = jnp.concatenate([filters, filters], axis=1)
        product = lax.dot_general(
            signal, filters, (((1,), (1,)), ((), ())), preferred_element_type=jnp.float32
        )
        total = product[0:COARSE]
        for m in range(1, count):
            part = product[m * COARSE : (m + 1) * COARSE]
            part = jnp.where(wide_lane >= FINE * m, part, 0.0)
            total = total + pltpu.roll(part, width - FINE * m, 1)
        for group in range(width // LANES):
            block[group, pl.ds(at, COARSE, stride=CHUNK), :] = total[
                :, group * LANES : (group + 1) * LANES
            ]

    for turn in range(chunks):
        if turn < filter_turns:
            for step in order:
                forward(1, step, turn).wait_recv()
        elif shared:
            spread(turn).wait_recv()
        if shared and turn == 0:
            for other in range(1, groups):
                spread(other).start()
        for step in order:
            forward(0, step, turn).wait_recv()
        chunk = group_at(turn, 1)
        lax.fori_loop(0, CHUNK // TOGETHER, functools.partial(convolve, chunk), 0)
        for group in range(width // LANES):
            turned[turn, group * LANES : (group + 1) * LANES, :] = block[group].T
        for step in order:
            backward(step, turn).start()
        back[chunk * devices + me] = turned[turn, owner_rows(me), :]

    parts = LANES // CHUNK

    def store(group):
        target = pl.ds(pl.multiple_of(group * LANES, LANES), LANES)
        return pltpu.make_async_copy(
            placed.at[group], result.at[:, target], placed_sem.at[group]
        )

    def place(group, carry):
        for a in range(COARSE):
            lanes = pl.ds(a * CHUNK, CHUNK)
            merged = jnp.concatenate(
                [back[group * parts + part, :, lanes] for part in range(parts)], axis=1
            )
            for u in range(per_owner):
                start = LANES * (per_owner - 1 - u) + FINE * (COARSE - 1 - a)
                placed[group, start : start + FINE, :] = merged[u * FINE : (u + 1) * FINE]
        store(group).start()
        return carry

    for turn in range(chunks):
        for step in order:
            backward(step, turn).wait_recv()
        first = group_at(turn, 1) * (reach // LANES)
        lax.fori_loop(first, first + reach // LANES, place, 0)
    for turn in range(chunks):
        for step in order:
            forward(0, step, turn).wait_send()
            if turn < filter_turns:
                forward(1, step, turn).wait_send()
            backward(step, turn).wait_send()
    if shared:
        for turn in range(1, groups):
            spread(turn).wait_send()
    for group in range(channels // LANES):
        store(group).wait()


def local(in_gate, values, out_gate, filter_taps, skip_gain):
    own, channels = in_gate.shape
    devices = lax.axis_size("seq")
    groups = lax.axis_size("grp")
    share = channels // devices
    chunks = share // CHUNK
    width = FINE * (own // LANES) * devices
    owned = FINE * (own // LANES)
    pieces = pltpu.SemaphoreType.DMA((devices, chunks))
    conv = pl.pallas_call(
        functools.partial(kernel, devices, groups),
        out_shape=jax.ShapeDtypeStruct((own, channels), jnp.float32),
        in_specs=[pl.BlockSpec(memory_space=pl.ANY)] * 3,
        out_specs=pl.BlockSpec(memory_space=pl.ANY),
        scratch_shapes=[
            pltpu.VMEM((own, channels), jnp.bfloat16),
            pltpu.VMEM((own, channels), jnp.bfloat16),
            pltpu.VMEM((own, channels), jnp.bfloat16),
            pltpu.VMEM((2, own // LANES, channels, LANES), jnp.float32),
            pltpu.VMEM((devices, own // LANES, share, LANES), jnp.float32),
            pltpu.VMEM((devices, own // LANES, share, LANES), jnp.float32),
            pltpu.VMEM((width // LANES, COARSE * CHUNK, LANES), jnp.float32),
            pltpu.VMEM((chunks, width, COARSE * CHUNK), jnp.float32),
            pltpu.VMEM((devices * chunks, owned, COARSE * CHUNK), jnp.float32),
            pieces,
            pieces,
            pieces,
            pieces,
            pltpu.SemaphoreType.DMA((groups,)),
            pltpu.SemaphoreType.DMA((groups,)),
            pieces,
            pieces,
            pltpu.SemaphoreType.DMA((3,)),
            pltpu.VMEM((channels // LANES, own, LANES), jnp.float32),
            pltpu.SemaphoreType.DMA((channels // LANES,)),
        ],
        compiler_params=pltpu.CompilerParams(
            collective_id=0, has_side_effects=True, vmem_limit_bytes=60 * 1024 * 1024
        ),
    )(in_gate, values, filter_taps)
    gated = in_gate.astype(jnp.float32) * values.astype(jnp.float32)
    total = conv + skip_gain[None, :] * gated
    return (out_gate.astype(jnp.float32) * total).astype(jnp.bfloat16)


def solution(mesh):
    in_specs = (
        P(("grp", "seq"), None),
        P(("grp", "seq"), None),
        P(("grp", "seq"), None),
        P("seq", None),
        P(),
    )
    out_specs = P(("grp", "seq"), None)
    return jax.shard_map(local, mesh=mesh, in_specs=in_specs, out_specs=out_specs, check_vma=False)
```

```python
import functools

import jax
import jax.numpy as jnp
from jax import lax
from jax.experimental import pallas as pl
from jax.experimental.pallas import tpu as pltpu
from jax.sharding import PartitionSpec as P

LANES = 128
COARSE = 8
FINE = 16
CHUNK = 16
TOGETHER = 4


def kernel(
    devices,
    groups,
    in_gate_hbm,
    values_hbm,
    taps_hbm,
    result,
    in_gate,
    values,
    taps,
    sent,
    signals,
    filters_held,
    block,
    turned,
    back,
    signal_send,
    signal_recv,
    filter_send,
    filter_recv,
    spread_send,
    spread_recv,
    back_send,
    back_recv,
    load_sem,
    placed,
    placed_sem,
):
    loads = [
        pltpu.make_async_copy(source, target, load_sem.at[at])
        for at, (source, target) in enumerate(
            [
                (in_gate_hbm, in_gate),
                (values_hbm, values),
                (taps_hbm, taps),
            ]
        )
    ]
    for load in loads:
        load.start()
    own, channels = in_gate.shape
    share = channels // devices
    chunks = share // CHUNK
    per_owner = own // LANES
    count = per_owner * devices
    width = FINE * count
    me = lax.axis_index("seq")
    mine = lax.axis_index("grp")
    half = devices // 2
    order = [step for at in range(half) for step in (half + at, 1 + at)][: devices - 1]

    def partner(step):
        peer, bit = me * 0, 1
        while bit < devices:
            own_bit = lax.rem(lax.div(me, bit), 2)
            peer = peer + bit * (1 - own_bit if step & bit else own_bit)
            bit *= 2
        return peer

    shared = chunks == groups and groups % 2 == 0
    pairs = max(groups // 2, 1)

    def group_at(turn, sign):
        if not shared:
            return turn
        pair = lax.rem(lax.div(mine, 2) + sign * (turn // 2) + pairs, pairs)
        return 2 * pair + lax.rem(lax.rem(mine, 2) + turn % 2, 2)

    barrier = pltpu.get_barrier_semaphore()
    for step in order:
        peer = partner(step)
        pl.semaphore_signal(
            barrier, inc=1, device_id={"seq": peer}, device_id_type=pl.DeviceIdType.MESH
        )
    greeted = devices - 1
    if shared:
        for turn in range(1, groups):
            pl.semaphore_signal(
                barrier,
                inc=1,
                device_id={"grp": group_at(turn, 1)},
                device_id_type=pl.DeviceIdType.MESH,
            )
        greeted += groups - 1

    reach = devices * CHUNK

    def columns_of(chunk):
        return pl.ds(pl.multiple_of(chunk * reach, LANES), reach)

    def turn_signal(turn):
        columns = columns_of(group_at(turn, 1))
        gated = in_gate[:, columns].astype(jnp.float32) * values[:, columns].astype(jnp.float32)
        gated = gated.T
        for u in range(per_owner):
            sent[0, u, columns, :] = gated[:, u * LANES : (u + 1) * LANES]

    def turn_filter(turn):
        columns = columns_of(group_at(turn, 1))
        flip = (
            lax.broadcasted_iota(jnp.int32, (own, own), 0)
            + lax.broadcasted_iota(jnp.int32, (own, own), 1)
            == own - 1
        )
        flip = flip.astype(jnp.float32).astype(jnp.bfloat16)
        turned_taps = taps[:, columns].astype(jnp.float32).T.astype(jnp.bfloat16)
        turned_taps = jnp.dot(turned_taps, flip, preferred_element_type=jnp.float32)
        for u in range(per_owner):
            sent[1, u, columns, :] = turned_taps[:, u * LANES : (u + 1) * LANES]

    loads[0].wait()
    loads[1].wait()
    turn_signal(0)

    pl.semaphore_wait(barrier, greeted)

    def rows_of(device, chunk):
        return pl.ds(pl.multiple_of((chunk * devices + device) * CHUNK, CHUNK), CHUNK)

    def rows_in(chunk):
        return pl.ds(pl.multiple_of(chunk * CHUNK, CHUNK), CHUNK)

    def forward(which, step, turn):
        peer = partner(step)
        chunk = group_at(turn, 1)
        return pltpu.make_async_remote_copy(
            src_ref=sent.at[which, :, rows_of(peer, chunk), :],
            dst_ref=(signals, filters_held)[which].at[me, :, rows_in(chunk), :],
            send_sem=(signal_send, filter_send)[which].at[step, turn],
            recv_sem=(signal_recv, filter_recv)[which].at[step, turn],
            device_id={"seq": peer},
            device_id_type=pl.DeviceIdType.MESH,
        )

    def spread(turn):
        region = filters_held.at[:, :, rows_in(group_at(0, 1)), :]
        return pltpu.make_async_remote_copy(
            src_ref=region,
            dst_ref=region,
            send_sem=spread_send.at[turn],
            recv_sem=spread_recv.at[turn],
            device_id={"grp": group_at(turn, -1)},
            device_id_type=pl.DeviceIdType.MESH,
        )

    def owner_rows(device):
        start = FINE * per_owner * (devices - 1 - device)
        return pl.ds(pl.multiple_of(start, FINE * per_owner), FINE * per_owner)

    def backward(step, turn):
        peer = partner(step)
        return pltpu.make_async_remote_copy(
            src_ref=turned.at[turn, owner_rows(peer), :],
            dst_ref=back.at[group_at(turn, 1) * devices + me],
            send_sem=back_send.at[step, turn],
            recv_sem=back_recv.at[step, turn],
            device_id={"seq": peer},
            device_id_type=pl.DeviceIdType.MESH,
        )

    filter_turns = 1 if shared else chunks
    for turn in range(chunks):
        if turn > 0:
            turn_signal(turn)
        for step in order:
            forward(0, step, turn).start()
        if turn < filter_turns:
            if turn == 0:
                loads[2].wait()
            turn_filter(turn)
            for step in order:
                forward(1, step, turn).start()
    for turn in range(chunks):
        chunk = group_at(turn, 1)
        signals[me, :, rows_in(chunk), :] = sent[0, :, rows_of(me, chunk), :]
        if turn < filter_turns:
            filters_held[me, :, rows_in(chunk), :] = sent[1, :, rows_of(me, chunk), :]

    coarse_row = lax.broadcasted_iota(jnp.int32, (COARSE, LANES), 0)
    coarse_lane = lax.broadcasted_iota(jnp.int32, (COARSE, LANES), 1)
    coarse_mask = coarse_lane >= FINE * coarse_row
    fine_row = lax.broadcasted_iota(jnp.int32, (FINE, LANES), 0)
    fine_lane = lax.broadcasted_iota(jnp.int32, (FINE, LANES), 1)
    fine_mask = fine_lane + (FINE - 1) - fine_row < LANES
    wide_lane = lax.broadcasted_iota(jnp.int32, (COARSE, width), 1)

    def convolve(chunk, few, carry):
        for lane in range(TOGETHER):
            convolve_one(chunk, few * TOGETHER + lane)
        return carry

    def convolve_one(chunk, at):
        row = pl.ds(chunk * CHUNK + at, 1)
        pieces = []
        before = jnp.zeros((COARSE, LANES), jnp.float32)
        for m in range(count):
            line = signals[m // per_owner, m % per_owner, row, :]
            rolled = pltpu.roll(
                jnp.broadcast_to(line, (COARSE, LANES)), 0, 1, stride=FINE, stride_axis=0
            )
            shifted = jnp.where(coarse_mask, rolled, before)
            before = rolled
            pieces.append(shifted)
        signal = jnp.concatenate(pieces, axis=0)
        high = signal.astype(jnp.bfloat16)
        low = (signal - high.astype(jnp.float32)).astype(jnp.bfloat16)
        signal = jnp.concatenate([high, low], axis=1)
        pieces = []
        after = jnp.zeros((FINE, LANES), jnp.float32)
        for b in range(count - 1, -1, -1):
            line = filters_held[devices - 1 - b // per_owner, b % per_owner, row, :]
            rolled = pltpu.roll(
                jnp.broadcast_to(line, (FINE, LANES)),
                LANES - FINE + 1,
                1,
                stride=1,
                stride_axis=0,
            )
            pieces.append(jnp.where(fine_mask, rolled, after))
            after = rolled
        filters = jnp.concatenate(pieces[::-1], axis=0).astype(jnp.bfloat16)
        filters = jnp.concatenate([filters, filters], axis=1)
        product = lax.dot_general(
            signal, filters, (((1,), (1,)), ((), ())), preferred_element_type=jnp.float32
        )
        total = product[0:COARSE]
        for m in range(1, count):
            part = product[m * COARSE : (m + 1) * COARSE]
            part = jnp.where(wide_lane >= FINE * m, part, 0.0)
            total = total + pltpu.roll(part, width - FINE * m, 1)
        for group in range(width // LANES):
            block[group, pl.ds(at, COARSE, stride=CHUNK), :] = total[
                :, group * LANES : (group + 1) * LANES
            ]

    for turn in range(chunks):
        if turn < filter_turns:
            for step in order:
                forward(1, step, turn).wait_recv()
        elif shared:
            spread(turn).wait_recv()
        if shared and turn == 0:
            for other in range(1, groups):
                spread(other).start()
        for step in order:
            forward(0, step, turn).wait_recv()
        chunk = group_at(turn, 1)
        lax.fori_loop(0, CHUNK // TOGETHER, functools.partial(convolve, chunk), 0)
        for group in range(width // LANES):
            turned[turn, group * LANES : (group + 1) * LANES, :] = block[group].T
        for step in order:
            backward(step, turn).start()
        back[chunk * devices + me] = turned[turn, owner_rows(me), :]

    parts = LANES // CHUNK

    def store(group):
        target = pl.ds(pl.multiple_of(group * LANES, LANES), LANES)
        return pltpu.make_async_copy(
            placed.at[group], result.at[:, target], placed_sem.at[group]
        )

    def place(group, carry):
        for a in range(COARSE):
            lanes = pl.ds(a * CHUNK, CHUNK)
            merged = jnp.concatenate(
                [back[group * parts + part, :, lanes] for part in range(parts)], axis=1
            )
            for u in range(per_owner):
                start = LANES * (per_owner - 1 - u) + FINE * (COARSE - 1 - a)
                placed[group, start : start + FINE, :] = merged[u * FINE : (u + 1) * FINE]
        store(group).start()
        return carry

    for turn in range(chunks):
        for step in order:
            backward(step, turn).wait_recv()
        first = group_at(turn, 1) * (reach // LANES)
        lax.fori_loop(first, first + reach // LANES, place, 0)
    for turn in range(chunks):
        for step in order:
            forward(0, step, turn).wait_send()
            if turn < filter_turns:
                forward(1, step, turn).wait_send()
            backward(step, turn).wait_send()
    if shared:
        for turn in range(1, groups):
            spread(turn).wait_send()
    for group in range(channels // LANES):
        store(group).wait()


def local(in_gate, values, out_gate, filter_taps, skip_gain):
    own, channels = in_gate.shape
    devices = lax.axis_size("seq")
    groups = lax.axis_size("grp")
    share = channels // devices
    chunks = share // CHUNK
    width = FINE * (own // LANES) * devices
    owned = FINE * (own // LANES)
    pieces = pltpu.SemaphoreType.DMA((devices, chunks))
    conv = pl.pallas_call(
        functools.partial(kernel, devices, groups),
        out_shape=jax.ShapeDtypeStruct((own, channels), jnp.float32),
        in_specs=[pl.BlockSpec(memory_space=pl.ANY)] * 3,
        out_specs=pl.BlockSpec(memory_space=pl.ANY),
        scratch_shapes=[
            pltpu.VMEM((own, channels), jnp.bfloat16),
            pltpu.VMEM((own, channels), jnp.bfloat16),
            pltpu.VMEM((own, channels), jnp.bfloat16),
            pltpu.VMEM((2, own // LANES, channels, LANES), jnp.float32),
            pltpu.VMEM((devices, own // LANES, share, LANES), jnp.float32),
            pltpu.VMEM((devices, own // LANES, share, LANES), jnp.float32),
            pltpu.VMEM((width // LANES, COARSE * CHUNK, LANES), jnp.float32),
            pltpu.VMEM((chunks, width, COARSE * CHUNK), jnp.float32),
            pltpu.VMEM((devices * chunks, owned, COARSE * CHUNK), jnp.float32),
            pieces,
            pieces,
            pieces,
            pieces,
            pltpu.SemaphoreType.DMA((groups,)),
            pltpu.SemaphoreType.DMA((groups,)),
            pieces,
            pieces,
            pltpu.SemaphoreType.DMA((3,)),
            pltpu.VMEM((channels // LANES, own, LANES), jnp.float32),
            pltpu.SemaphoreType.DMA((channels // LANES,)),
        ],
        compiler_params=pltpu.CompilerParams(
            collective_id=0, has_side_effects=True, vmem_limit_bytes=60 * 1024 * 1024
        ),
    )(in_gate, values, filter_taps)
    gated = in_gate.astype(jnp.float32) * values.astype(jnp.float32)
    total = conv + skip_gain[None, :] * gated
    return (out_gate.astype(jnp.float32) * total).astype(jnp.bfloat16)


def solution(mesh):
    in_specs = (
        P(("grp", "seq"), None),
        P(("grp", "seq"), None),
        P(("grp", "seq"), None),
        P("seq", None),
        P(),
    )
    out_specs = P(("grp", "seq"), None)
    return jax.shard_map(local, mesh=mesh, in_specs=in_specs, out_specs=out_specs, check_vma=False)
```

```python
import functools

import jax
import jax.numpy as jnp
from jax import lax
from jax.experimental import pallas as pl
from jax.experimental.pallas import tpu as pltpu
from jax.sharding import PartitionSpec as P

LANES = 128
COARSE = 8
FINE = 16
CHUNK = 16
TOGETHER = 4


def kernel(
    devices,
    groups,
    in_gate_hbm,
    values_hbm,
    taps_hbm,
    result,
    in_gate,
    values,
    taps,
    sent,
    signals,
    filters_held,
    block,
    turned,
    back,
    signal_send,
    signal_recv,
    filter_send,
    filter_recv,
    spread_send,
    spread_recv,
    back_send,
    back_recv,
    load_sem,
    placed,
    placed_sem,
):
    loads = [
        pltpu.make_async_copy(source, target, load_sem.at[at])
        for at, (source, target) in enumerate(
            [
                (in_gate_hbm, in_gate),
                (values_hbm, values),
                (taps_hbm, taps),
            ]
        )
    ]
    for load in loads:
        load.start()
    own, channels = in_gate.shape
    share = channels // devices
    chunks = share // CHUNK
    per_owner = own // LANES
    count = per_owner * devices
    width = FINE * count
    me = lax.axis_index("seq")
    mine = lax.axis_index("grp")
    half = devices // 2
    order = [step for at in range(half) for step in (half + at, 1 + at)][: devices - 1]

    def partner(step):
        peer, bit = me * 0, 1
        while bit < devices:
            own_bit = lax.rem(lax.div(me, bit), 2)
            peer = peer + bit * (1 - own_bit if step & bit else own_bit)
            bit *= 2
        return peer

    shared = chunks == groups and groups % 2 == 0
    pairs = max(groups // 2, 1)

    def group_at(turn, sign):
        if not shared:
            return turn
        pair = lax.rem(lax.div(mine, 2) + sign * (turn // 2) + pairs, pairs)
        return 2 * pair + lax.rem(lax.rem(mine, 2) + turn % 2, 2)

    barrier = pltpu.get_barrier_semaphore()
    for step in order:
        peer = partner(step)
        pl.semaphore_signal(
            barrier, inc=1, device_id={"seq": peer}, device_id_type=pl.DeviceIdType.MESH
        )
    greeted = devices - 1
    if shared:
        for turn in range(1, groups):
            pl.semaphore_signal(
                barrier,
                inc=1,
                device_id={"grp": group_at(turn, 1)},
                device_id_type=pl.DeviceIdType.MESH,
            )
        greeted += groups - 1

    reach = devices * CHUNK

    def columns_of(chunk):
        return pl.ds(pl.multiple_of(chunk * reach, LANES), reach)

    def turn_signal(turn):
        columns = columns_of(group_at(turn, 1))
        gated = in_gate[:, columns].astype(jnp.float32) * values[:, columns].astype(jnp.float32)
        gated = gated.T
        for u in range(per_owner):
            sent[0, u, columns, :] = gated[:, u * LANES : (u + 1) * LANES]

    def turn_filter(turn):
        columns = columns_of(group_at(turn, 1))
        flip = (
            lax.broadcasted_iota(jnp.int32, (own, own), 0)
            + lax.broadcasted_iota(jnp.int32, (own, own), 1)
            == own - 1
        )
        flip = flip.astype(jnp.float32).astype(jnp.bfloat16)
        turned_taps = taps[:, columns].astype(jnp.float32).T.astype(jnp.bfloat16)
        turned_taps = jnp.dot(turned_taps, flip, preferred_element_type=jnp.float32)
        for u in range(per_owner):
            sent[1, u, columns, :] = turned_taps[:, u * LANES : (u + 1) * LANES]

    loads[0].wait()
    loads[1].wait()
    turn_signal(0)

    pl.semaphore_wait(barrier, greeted)

    def rows_of(device, chunk):
        return pl.ds(pl.multiple_of((chunk * devices + device) * CHUNK, CHUNK), CHUNK)

    def rows_in(chunk):
        return pl.ds(pl.multiple_of(chunk * CHUNK, CHUNK), CHUNK)

    def forward(which, step, turn):
        peer = partner(step)
        chunk = group_at(turn, 1)
        return pltpu.make_async_remote_copy(
            src_ref=sent.at[which, :, rows_of(peer, chunk), :],
            dst_ref=(signals, filters_held)[which].at[me, :, rows_in(chunk), :],
            send_sem=(signal_send, filter_send)[which].at[step, turn],
            recv_sem=(signal_recv, filter_recv)[which].at[step, turn],
            device_id={"seq": peer},
            device_id_type=pl.DeviceIdType.MESH,
        )

    def spread(turn):
        region = filters_held.at[:, :, rows_in(group_at(0, 1)), :]
        return pltpu.make_async_remote_copy(
            src_ref=region,
            dst_ref=region,
            send_sem=spread_send.at[turn],
            recv_sem=spread_recv.at[turn],
            device_id={"grp": group_at(turn, -1)},
            device_id_type=pl.DeviceIdType.MESH,
        )

    def owner_rows(device):
        start = FINE * per_owner * (devices - 1 - device)
        return pl.ds(pl.multiple_of(start, FINE * per_owner), FINE * per_owner)

    def backward(step, turn):
        peer = partner(step)
        return pltpu.make_async_remote_copy(
            src_ref=turned.at[turn, owner_rows(peer), :],
            dst_ref=back.at[group_at(turn, 1) * devices + me],
            send_sem=back_send.at[step, turn],
            recv_sem=back_recv.at[step, turn],
            device_id={"seq": peer},
            device_id_type=pl.DeviceIdType.MESH,
        )

    filter_turns = 1 if shared else chunks
    for turn in range(chunks):
        if turn > 0:
            turn_signal(turn)
        for step in order:
            forward(0, step, turn).start()
        if turn < filter_turns:
            if turn == 0:
                loads[2].wait()
            turn_filter(turn)
            for step in order:
                forward(1, step, turn).start()
    for turn in range(chunks):
        chunk = group_at(turn, 1)
        signals[me, :, rows_in(chunk), :] = sent[0, :, rows_of(me, chunk), :]
        if turn < filter_turns:
            filters_held[me, :, rows_in(chunk), :] = sent[1, :, rows_of(me, chunk), :]

    coarse_row = lax.broadcasted_iota(jnp.int32, (COARSE, LANES), 0)
    coarse_lane = lax.broadcasted_iota(jnp.int32, (COARSE, LANES), 1)
    coarse_mask = coarse_lane >= FINE * coarse_row
    fine_row = lax.broadcasted_iota(jnp.int32, (FINE, LANES), 0)
    fine_lane = lax.broadcasted_iota(jnp.int32, (FINE, LANES), 1)
    fine_mask = fine_lane + (FINE - 1) - fine_row < LANES
    wide_lane = lax.broadcasted_iota(jnp.int32, (COARSE, width), 1)

    def convolve(chunk, few, carry):
        for lane in range(TOGETHER):
            convolve_one(chunk, few * TOGETHER + lane)
        return carry

    def convolve_one(chunk, at):
        row = pl.ds(chunk * CHUNK + at, 1)
        pieces = []
        before = jnp.zeros((COARSE, LANES), jnp.float32)
        for m in range(count):
            line = signals[m // per_owner, m % per_owner, row, :]
            rolled = pltpu.roll(
                jnp.broadcast_to(line, (COARSE, LANES)), 0, 1, stride=FINE, stride_axis=0
            )
            shifted = jnp.where(coarse_mask, rolled, before)
            before = rolled
            pieces.append(shifted)
        signal = jnp.concatenate(pieces, axis=0)
        high = signal.astype(jnp.bfloat16)
        low = (signal - high.astype(jnp.float32)).astype(jnp.bfloat16)
        signal = jnp.concatenate([high, low], axis=1)
        pieces = []
        after = jnp.zeros((FINE, LANES), jnp.float32)
        for b in range(count - 1, -1, -1):
            line = filters_held[devices - 1 - b // per_owner, b % per_owner, row, :]
            rolled = pltpu.roll(
                jnp.broadcast_to(line, (FINE, LANES)),
                LANES - FINE + 1,
                1,
                stride=1,
                stride_axis=0,
            )
            pieces.append(jnp.where(fine_mask, rolled, after))
            after = rolled
        filters = jnp.concatenate(pieces[::-1], axis=0).astype(jnp.bfloat16)
        filters = jnp.concatenate([filters, filters], axis=1)
        product = lax.dot_general(
            signal, filters, (((1,), (1,)), ((), ())), preferred_element_type=jnp.float32
        )
        total = product[0:COARSE]
        for m in range(1, count):
            part = product[m * COARSE : (m + 1) * COARSE]
            part = jnp.where(wide_lane >= FINE * m, part, 0.0)
            total = total + pltpu.roll(part, width - FINE * m, 1)
        for group in range(width // LANES):
            block[group, pl.ds(at, COARSE, stride=CHUNK), :] = total[
                :, group * LANES : (group + 1) * LANES
            ]

    for turn in range(chunks):
        if turn < filter_turns:
            for step in order:
                forward(1, step, turn).wait_recv()
        elif shared:
            spread(turn).wait_recv()
        if shared and turn == 0:
            for other in range(1, groups):
                spread(other).start()
        for step in order:
            forward(0, step, turn).wait_recv()
        chunk = group_at(turn, 1)
        lax.fori_loop(0, CHUNK // TOGETHER, functools.partial(convolve, chunk), 0)
        for group in range(width // LANES):
            turned[turn, group * LANES : (group + 1) * LANES, :] = block[group, : COARSE * CHUNK].T
        for step in order:
            backward(step, turn).start()
        back[chunk * devices + me] = turned[turn, owner_rows(me), :]

    parts = LANES // CHUNK

    def store(group):
        target = pl.ds(pl.multiple_of(group * LANES, LANES), LANES)
        return pltpu.make_async_copy(
            placed.at[group], result.at[:, target], placed_sem.at[group]
        )

    def place(group, carry):
        for a in range(COARSE):
            lanes = pl.ds(a * CHUNK, CHUNK)
            merged = jnp.concatenate(
                [back[group * parts + part, :, lanes] for part in range(parts)], axis=1
            )
            for u in range(per_owner):
                start = LANES * (per_owner - 1 - u) + FINE * (COARSE - 1 - a)
                placed[group, start : start + FINE, :] = merged[u * FINE : (u + 1) * FINE]
        store(group).start()
        return carry

    for turn in range(chunks):
        for step in order:
            backward(step, turn).wait_recv()
        first = group_at(turn, 1) * (reach // LANES)
        lax.fori_loop(first, first + reach // LANES, place, 0)
    for turn in range(chunks):
        for step in order:
            forward(0, step, turn).wait_send()
            if turn < filter_turns:
                forward(1, step, turn).wait_send()
            backward(step, turn).wait_send()
    if shared:
        for turn in range(1, groups):
            spread(turn).wait_send()
    for group in range(channels // LANES):
        store(group).wait()


def local(in_gate, values, out_gate, filter_taps, skip_gain):
    own, channels = in_gate.shape
    devices = lax.axis_size("seq")
    groups = lax.axis_size("grp")
    share = channels // devices
    chunks = share // CHUNK
    width = FINE * (own // LANES) * devices
    owned = FINE * (own // LANES)
    pieces = pltpu.SemaphoreType.DMA((devices, chunks))
    conv = pl.pallas_call(
        functools.partial(kernel, devices, groups),
        out_shape=jax.ShapeDtypeStruct((own, channels), jnp.float32),
        in_specs=[pl.BlockSpec(memory_space=pl.ANY)] * 3,
        out_specs=pl.BlockSpec(memory_space=pl.ANY),
        scratch_shapes=[
            pltpu.VMEM((own, channels), jnp.bfloat16),
            pltpu.VMEM((own, channels), jnp.bfloat16),
            pltpu.VMEM((own, channels), jnp.bfloat16),
            pltpu.VMEM((2, own // LANES, channels, LANES), jnp.float32),
            pltpu.VMEM((devices, own // LANES, share, LANES), jnp.float32),
            pltpu.VMEM((devices, own // LANES, share, LANES), jnp.float32),
            pltpu.VMEM((width // LANES, (COARSE + 1) * CHUNK, LANES), jnp.float32),
            pltpu.VMEM((chunks, width, COARSE * CHUNK), jnp.float32),
            pltpu.VMEM((devices * chunks, owned, COARSE * CHUNK), jnp.float32),
            pieces,
            pieces,
            pieces,
            pieces,
            pltpu.SemaphoreType.DMA((groups,)),
            pltpu.SemaphoreType.DMA((groups,)),
            pieces,
            pieces,
            pltpu.SemaphoreType.DMA((3,)),
            pltpu.VMEM((channels // LANES, own, LANES), jnp.float32),
            pltpu.SemaphoreType.DMA((channels // LANES,)),
        ],
        compiler_params=pltpu.CompilerParams(
            collective_id=0, has_side_effects=True, vmem_limit_bytes=60 * 1024 * 1024
        ),
    )(in_gate, values, filter_taps)
    gated = in_gate.astype(jnp.float32) * values.astype(jnp.float32)
    total = conv + skip_gain[None, :] * gated
    return (out_gate.astype(jnp.float32) * total).astype(jnp.bfloat16)


def solution(mesh):
    in_specs = (
        P(("grp", "seq"), None),
        P(("grp", "seq"), None),
        P(("grp", "seq"), None),
        P("seq", None),
        P(),
    )
    out_specs = P(("grp", "seq"), None)
    return jax.shard_map(local, mesh=mesh, in_specs=in_specs, out_specs=out_specs, check_vma=False)
```
